32 devices in a mesh: group: 2 (over x), tp: 16 (over z, y, core).
Axes of the slice: x: 2, y: 2, z: 4, core: 2. Of those that a mesh axis runs over, the one named last changes fastest.
Arguments:
- hidden_in: bfloat16 [256, 12288], P(('group', 'tp')), parts along dimension 0, may hold values from -6 to 6
- norm_gain: float32 [12288], replicated, may hold values from 0.1 to 1.9
- norm_shift: float32 [12288], replicated, may hold values from -3 to 3
- up_weight: bfloat16 [12288, 32768], P(None, 'tp'), may hold values from -0.0546875 to 0.0546875
- up_bias: bfloat16 [32768], P('tp'), may hold values from -3 to 3
- down_weight: bfloat16 [32768, 12288], P('tp'), may hold values from -0.09375 to 0.09375
- down_bias: float32 [12288], replicated, may hold values from -3 to 3
- active: int32 [256, 32], P(('group', 'tp')), parts along dimension 0, may hold values from 0 to 255, all different within a row; in each aligned block of 8 rows (0 to 7, 8 to 15, ...) at most 2 rows name the same one
Outputs:
- mixed: bfloat16 [256, 12288], P(('group', 'tp')), parts along dimension 0
The draws below stay inside these ranges and needn't reach their ends.
There are 2 independent parts, one for each index of `group`. The reference program is written for one: setup_inputs(seed, part) draws one part's arguments, and reference() takes and returns one part's arrays. A program takes and returns all parts, laid end to end along the dimension named above; an argument that names none is the same for every part. Nothing has to cross between parts.
Inputs may be any that keep to these rules, and one draw needn't show every extreme that they name: `active`: each row names 32 different blocks; among the 8 rows of one device no block is named by more than 2 rows, and some block is named by exactly 2 of them.
All inputs are finite; a program needn't handle non-finite values.
Results may differ from the reference program's by a relative error of at most 0.0075.
Values may be sent and summed in bfloat16 or wider, within the bound.
A program may use at most 256 MiB of HBM per device.

```python
import math
import jax
import jax.numpy as jnp
import numpy as np
from jax import lax

D = 12288
FF = 32768
BLOCK = 128
K = 32
TOK_DEV = 8
NB = 256
CAP = 2
TOKENS = 128


def shard_levels(own_key, shape, cuts, least, high):
    def one(position, shards_of):
        draws = jax.random.uniform(jax.random.fold_in(jax.random.fold_in(own_key, 6), position), (shards_of,), jnp.float32, least / len(cuts), high / len(cuts))
        return jnp.repeat(jnp.exp(draws), shape[position] // shards_of).reshape((-1,) + (1,) * (len(shape) - position - 1))

    gain = one(*cuts[0])
    for cut in cuts[1:]:
        gain = gain * one(*cut)
    return gain


def deal_out(key, own, number, rows, count, top, reach, skew):
    order = jax.random.permutation(key, count)
    crowded, usual = portions_of(count, rows * top, reach, skew, True), portions_of(count, rows * top, reach, skew, False)
    places = jnp.arange(count)

    def named(sizes, rotation):
        used = int((sizes > 0).sum())
        fixed = max(1, used // 4)
        moved = fixed + (places - fixed + rotation * (used - fixed)) % max(1, count - fixed)
        return jnp.zeros((count,), jnp.int32).at[order[jnp.where(places < fixed, places, moved)]].set(jnp.asarray(sizes, jnp.int32))

    sizes = jnp.where(number % 4 == 0, named(crowded, number // 4), named(usual, number - number // 4 - 1))
    mixed = jax.random.permutation(jax.random.fold_in(own, 3), count)
    giver, receiver = mixed[0:count // 2 * 2:2], mixed[1:count // 2 * 2:2]
    slack = jnp.minimum(sizes[giver] - 1, reach - sizes[receiver]) // 2
    slack = jnp.where((giver == order[0]) | (receiver == order[0]) | (sizes[receiver] == 0), 0, jnp.maximum(slack, 0))
    moved = jax.random.randint(jax.random.fold_in(own, 4), (count // 2,), 0, 1 << 20) % (slack + 1)
    sizes = sizes.at[giver].add(-moved).at[receiver].add(moved)
    items = jnp.searchsorted(jnp.cumsum(sizes), jnp.arange(rows * top), side="right").astype(jnp.int32)
    grid = items.reshape(top, rows).T
    grid = grid[jax.random.permutation(jax.random.fold_in(own, 1), rows)]
    rotation = jax.random.randint(jax.random.fold_in(own, 2), (rows, 1), 0, top)
    return jnp.take_along_axis(grid, (jnp.arange(top)[None, :] + rotation) % top, axis=1)


def portions_of(number_of, total, reach, slope, full):
    portions = [(1 << 20) // math.isqrt(rank ** slope) + 1 for rank in range(1, number_of + 1)]
    largest = reach if full else min(reach, max(-(-total // number_of), total * portions[0] // sum(portions)))
    least = 1 if total - largest >= number_of - 1 else 0
    holding, surplus = [largest] + [least] * (number_of - 1), total - largest - least * (number_of - 1)
    while surplus > 0:
        movable = [i for i in range(1, number_of) if holding[i] < largest] or [i for i in range(1, number_of) if holding[i] < reach]
        mass, remaining = sum([portions[i] for i in movable]), surplus
        for i in movable:
            more = min(reach - holding[i], max(1, remaining * portions[i] // mass), surplus)
            holding[i] = holding[i] + more
            surplus = surplus - more
    return np.array(holding)


def centred(key, shape, deviation, most, cuts=(), dtype=jnp.bfloat16):
    result = deviation * jax.random.normal(key, shape, jnp.float32)
    if cuts:
        result = result * shard_levels(key, shape, cuts, -0.22, 0.18)
    return jnp.clip(result, -most, most).astype(dtype)


def setup_inputs(seed: int = 0, part: int = 0) -> dict:
    splits = jax.random.split(jax.random.key(seed), 9)
    part_splits = jax.random.split(jax.random.fold_in(splits[8], part), 9)
    hidden_in = centred(part_splits[0], (TOKENS, D), 1.0, 6.0, ((0, 16),))
    norm_gain = jnp.clip(1.0 + 0.18 * jax.random.normal(splits[1], (D,), jnp.float32), 0.1, 1.9)
    norm_shift = centred(splits[2], (D,), 0.5, 3.0, (), jnp.float32)
    up_weight = centred(splits[3], (D, FF), D ** -0.5, 0.0546875, ((1, 16),))
    up_bias = centred(splits[4], (FF,), 0.5, 3.0, ((0, 16),))
    down_weight = centred(splits[5], (FF, D), (K * BLOCK) ** -0.5, 0.09375, ((0, 16),))
    down_bias = centred(splits[6], (D,), 0.5, 3.0, (), jnp.float32)
    active_keys = jax.random.split(jax.random.fold_in(part_splits[7], 1), TOKENS // TOK_DEV)
    active_turns = jax.random.permutation(jax.random.fold_in(part_splits[7], 3), TOKENS // TOK_DEV)
    active = jax.vmap(lambda own, number: deal_out(jax.random.fold_in(part_splits[7], 2), own, number, TOK_DEV, NB, K, CAP, 2))(active_keys, active_turns).reshape((TOKENS, K))
    return dict(hidden_in=hidden_in, norm_gain=norm_gain, norm_shift=norm_shift, up_weight=up_weight, up_bias=up_bias, down_weight=down_weight, down_bias=down_bias, active=active)


def layer_norm(hidden_in, norm_gain, norm_shift):
    values = hidden_in.astype(jnp.float32)
    center = lax.optimization_barrier(jnp.mean(values, axis=1, keepdims=True))
    spread = lax.optimization_barrier(jnp.mean((values - center) ** 2, axis=1, keepdims=True))
    scaled = (values - center) / jnp.sqrt(spread + 1e-05)
    return (scaled * norm_gain + norm_shift).astype(jnp.bfloat16)

def reference(hidden_in, norm_gain, norm_shift, up_weight, up_bias, down_weight, down_bias, active):
    normed = layer_norm(hidden_in, norm_gain, norm_shift)
    up_blocks = up_weight.reshape(D, NB, BLOCK)
    bias_blocks = up_bias.reshape(NB, BLOCK)
    down_blocks = down_weight.reshape(NB, BLOCK, D)

    def one_row(pair):
        row_vec, block_ids = pair
        block_ids = block_ids.astype(jnp.int32)
        gathered_up = jnp.take(up_blocks, block_ids, axis=1).reshape(D, K * BLOCK)
        preact = jnp.dot(row_vec[None, :], gathered_up, preferred_element_type=jnp.float32)[0]
        preact = preact + jnp.take(bias_blocks, block_ids, axis=0).reshape(K * BLOCK).astype(jnp.float32)
        activated = jnp.maximum(preact, 0.0).astype(jnp.bfloat16).reshape(K, BLOCK)
        gathered_down = jnp.take(down_blocks, block_ids, axis=0).astype(jnp.float32)
        pieces = jnp.einsum('kj,kjd->kd', activated.astype(jnp.float32), gathered_down, precision=lax.Precision.HIGHEST).astype(jnp.bfloat16)
        return lax.optimization_barrier(jnp.sum(pieces.astype(jnp.float32), axis=0))
    summed = lax.map(one_row, (normed, active))
    return (summed + down_bias.astype(jnp.float32)).astype(jnp.bfloat16)
```

```python
import jax
import jax.numpy as jnp
from jax import lax
from jax.sharding import PartitionSpec as P

BLOCK = 128


def layer_norm(hidden_in, norm_gain, norm_shift):
    values = hidden_in.astype(jnp.float32)
    center = jnp.mean(values, axis=1, keepdims=True)
    spread = jnp.mean((values - center) ** 2, axis=1, keepdims=True)
    scaled = (values - center) / jnp.sqrt(spread + 1e-05)
    return (scaled * norm_gain + norm_shift).astype(jnp.bfloat16)


def per_device(
    hidden_in, norm_gain, norm_shift, up_weight, up_bias, down_weight, down_bias, active
):
    local_blocks = up_weight.shape[1] // BLOCK
    normed = layer_norm(hidden_in, norm_gain, norm_shift)
    rows = lax.all_gather(normed, "tp", axis=0, tiled=True)
    ids = lax.all_gather(active, "tp", axis=0, tiled=True)
    own = lax.axis_index("tp") * local_blocks + jnp.arange(local_blocks, dtype=jnp.int32)
    mask = jnp.any(ids[:, :, None] == own[None, None, :], axis=1)
    preact = jnp.dot(rows, up_weight, preferred_element_type=jnp.float32)
    preact = preact + up_bias.astype(jnp.float32)
    activated = jnp.maximum(preact, 0.0).astype(jnp.bfloat16)
    activated = jnp.where(jnp.repeat(mask, BLOCK, axis=1), activated, 0)
    part = jnp.dot(activated, down_weight, preferred_element_type=jnp.float32)
    summed = lax.psum_scatter(part.astype(jnp.bfloat16), "tp", scatter_dimension=0, tiled=True)
    return (summed.astype(jnp.float32) + down_bias).astype(jnp.bfloat16)


def solution(mesh):
    return jax.shard_map(
        per_device,
        mesh=mesh,
        in_specs=(
            P(("group", "tp"), None),
            P(),
            P(),
            P(None, "tp"),
            P("tp"),
            P("tp", None),
            P(),
            P(("group", "tp"), None),
        ),
        out_specs=P(("group", "tp"), None),
        check_vma=False,
    )
```

```python
import functools

import jax
import jax.numpy as jnp
from jax import lax
from jax.experimental import pallas as pl
from jax.experimental.pallas import tpu as pltpu
from jax.sharding import PartitionSpec as P

BLOCK = 128


def layer_norm(hidden_in, norm_gain, norm_shift):
    values = hidden_in.astype(jnp.float32)
    center = jnp.mean(values, axis=1, keepdims=True)
    spread = jnp.mean((values - center) ** 2, axis=1, keepdims=True)
    scaled = (values - center) / jnp.sqrt(spread + 1e-05)
    return (scaled * norm_gain + norm_shift).astype(jnp.bfloat16)


F32 = jnp.float32
BF16 = jnp.bfloat16
SLOTS = 10


def fused_kernel(
    dims, hidden, gain, shift, up_hbm, up_bias, down_hbm, down_bias, active, out,
    wbuf, xn, xs, ids_own, ids_sib, xg, idg, preact, act, part, pown,
    ssend, srecv, asend, arecv, bsend, brecv,
    w_sem, e_send, e_recv, ga_send, ga_recv, gb_send, gb_recv, gs_send, gs_recv,
    ia_send, ia_recv, ib_send, ib_recv, ra_send, ra_recv, rb_send, rb_recv, rs_send, rs_recv,
):
    chips, chunks, wide, slots = dims
    half = wide // 2
    hops_a, hops_b = chips // 2, chips - 1 - chips // 2
    deep = chips // 2
    me = lax.axis_index("tp")
    core = lax.rem(me, 2)
    chip = me // 2
    side = lax.rem(chip, 2)
    step_z = chip // 2
    pos = step_z + side * (2 * deep - 1 - 2 * step_z)
    turn = 1 - 2 * core

    def device_at(place):
        s = place // deep
        z = place + s * (2 * deep - 1 - 2 * place)
        return (z * 2 + s) * 2 + core

    def place_of(offset):
        return lax.rem(pos + turn * offset + 2 * chips, chips)

    to_a = device_at(place_of(1))
    to_b = device_at(place_of(-1))
    sibling = chip * 2 + 1 - core

    def send(src, dst, s_sem, r_sem, target):
        return pltpu.make_async_remote_copy(
            src_ref=src, dst_ref=dst, send_sem=s_sem, recv_sem=r_sem,
            device_id={"tp": target}, device_id_type=pl.DeviceIdType.MESH,
        )

    def block(place):
        return pl.ds(pl.multiple_of(place * 16, 16), 16)

    def w_up(g, slot, j):
        rows = pl.ds(pl.multiple_of(g * wide, wide), wide)
        return pltpu.make_async_copy(
            up_hbm.at[rows, pl.ds(j * wide, wide)],
            wbuf.at[slot, :, pl.ds(j * wide, wide)], w_sem.at[slot, j])

    def w_down(n, slot, j):
        cols = pl.ds(pl.multiple_of(n * wide, wide), wide)
        return pltpu.make_async_copy(
            down_hbm.at[pl.ds(j * wide, wide), cols],
            wbuf.at[slot, :, pl.ds(j * wide, wide)], w_sem.at[slot, j])

    def w_start(g):
        slot = lax.rem(g, slots)

        @pl.when(g < chunks)
        def _():
            w_up(g, slot, 0).start()
            w_up(g, slot, 1).start()

        @pl.when((g >= chunks) & (g < 2 * chunks))
        def _():
            w_down(g - chunks, slot, 0).start()
            w_down(g - chunks, slot, 1).start()

    for g in range(slots):
        for j in range(2):
            w_up(g, g, j).start()

    barrier = pltpu.get_barrier_semaphore()
    for other in (to_a, to_b, sibling):
        pl.semaphore_signal(
            barrier, inc=1, device_id={"tp": other}, device_id_type=pl.DeviceIdType.MESH)

    values = hidden[...].astype(F32)
    center = jnp.mean(values, axis=1, keepdims=True)
    spread = jnp.mean((values - center) ** 2, axis=1, keepdims=True)
    root = jnp.sqrt(spread + 1e-05)
    for k in range(chunks):
        for h in range(2):
            cols = slice(k * wide + h * half, k * wide + h * half + half)
            scaled = (hidden[:, cols].astype(F32) - center) / root
            xn[h, k] = (scaled * gain[:, cols] + shift[:, cols]).astype(BF16).astype(F32)
    ids_own[...] = jnp.full(ids_own.shape, -1.0, F32)
    ids_own[:, : active.shape[1]] = active[...].astype(F32)
    preact[...] = jnp.zeros(preact.shape, F32)
    pl.semaphore_wait(barrier, 3)
    swap_x = send(xn.at[1 - core], xs, e_send.at[0], e_recv.at[0], sibling)
    swap_i = send(ids_own, ids_sib, e_send.at[1], e_recv.at[1], sibling)
    swap_x.start()
    swap_i.start()
    swap_x.wait_recv()
    swap_i.wait_recv()

    def pair(mine, theirs):
        first = jnp.where(core == 0, mine, theirs)
        second = jnp.where(core == 0, theirs, mine)
        return jnp.concatenate([first, second], axis=0).astype(BF16)

    idg[block(pos), :] = pair(ids_own[...], ids_sib[...])

    def g_a(k, h):
        ref = xg.at[k, core, block(place_of(-(h - 1))), :]
        return send(ref, ref, ga_send.at[k, h - 1], ga_recv.at[k, h - 1], to_a)

    def g_b(k, h):
        ref = xg.at[k, core, block(place_of(h - 1)), :]
        return send(ref, ref, gb_send.at[k, h - 1], gb_recv.at[k, h - 1], to_b)

    def i_a(h):
        ref = idg.at[block(place_of(-(h - 1))), :]
        return send(ref, ref, ia_send.at[h - 1], ia_recv.at[h - 1], to_a)

    def i_b(h):
        ref = idg.at[block(place_of(h - 1)), :]
        return send(ref, ref, ib_send.at[h - 1], ib_recv.at[h - 1], to_b)

    def g_s(k):
        ref = xg.at[k, core]
        return send(ref, ref, gs_send.at[k], gs_recv.at[k], sibling)

    def gather_step(s, carry):
        @pl.when(s < chunks)
        def _():
            xg[s, core, block(pos), :] = pair(xn[core, s], xs[s])
            g_a(s, 1).start()
            g_b(s, 1).start()

        @pl.when(s == 0)
        def _():
            i_a(1).start()
            i_b(1).start()

        for h in range(1, hops_a + 1):
            k = s - h

            @pl.when((k >= 0) & (k < chunks))
            def _():
                g_a(k, h).wait_recv()
                if h < hops_a:
                    g_a(k, h + 1).start()
                if h <= hops_b:
                    g_b(k, h).wait_recv()
                if h < hops_b:
                    g_b(k, h + 1).start()
                if h == hops_a:
                    g_s(k).start()

            @pl.when(k == 0)
            def _():
                i_a(h).wait_recv()
                if h < hops_a:
                    i_a(h + 1).start()
                if h <= hops_b:
                    i_b(h).wait_recv()
                if h < hops_b:
                    i_b(h + 1).start()

        k = s - hops_a - 1

        @pl.when(k >= 0)
        def _():
            g_s(k).wait_recv()
            slot = lax.rem(k, slots)
            w_up(k, slot, 0).wait()
            w_up(k, slot, 1).wait()
            tile = min(512, wide)
            for j in range(0, 2 * wide, tile):
                cols = slice(j, j + tile)
                preact[:, cols] += jnp.dot(
                    xg[k, 0], wbuf[slot, :half, cols], preferred_element_type=F32
                ) + jnp.dot(xg[k, 1], wbuf[slot, half:, cols], preferred_element_type=F32)
            w_start(k + slots)

        return carry

    lax.fori_loop(0, chunks + hops_a + 1, gather_step, 0)

    ids = idg[...].astype(F32)
    for b in range(2 * wide // BLOCK):
        cols = slice(b * BLOCK, b * BLOCK + BLOCK)
        name = (me * (2 * wide // BLOCK) + b).astype(F32)
        named = jnp.max(jnp.where(ids == name, 1.0, 0.0), axis=1, keepdims=True)
        value = jnp.maximum(preact[:, cols] + up_bias[:, cols].astype(F32), 0.0)
        act[:, cols] = (value * named).astype(BF16)

    def r_s(n):
        return send(ssend.at[n], srecv.at[n], rs_send.at[n], rs_recv.at[n], sibling)

    def r_a(n, h):
        return send(asend.at[n, h - 1], arecv.at[n, h - 1], ra_send.at[n, h - 1],
                    ra_recv.at[n, h - 1], to_a)

    def r_b(n, h):
        return send(bsend.at[n, h - 1], brecv.at[n, h - 1], rb_send.at[n, h - 1],
                    rb_recv.at[n, h - 1], to_b)

    def scatter_step(s, carry):
        n = s - hops_a - 1

        @pl.when(n >= 0)
        def _():
            r_a(n, hops_a).wait_recv()
            r_b(n, hops_b).wait_recv()
            total = pown[n, block(pos), :] + arecv[n, hops_a - 1].astype(F32)
            total = total + brecv[n, hops_b - 1].astype(F32)
            for h in range(2):
                cols = pl.ds(pl.multiple_of(n * wide + h * half, half), half)
                out[:, cols] = (total[8 * h : 8 * h + 8] + down_bias[:, cols]).astype(BF16)

        for h in range(hops_a - 1, 0, -1):
            n = s - 1 - h

            @pl.when((n >= 0) & (n < chunks))
            def _():
                r_a(n, h).wait_recv()
                here = pown[n, block(place_of(hops_a - h)), :]
                asend[n, h] = (arecv[n, h - 1].astype(F32) + here).astype(BF16)
                r_a(n, h + 1).start()
                if h < hops_b:
                    r_b(n, h).wait_recv()
                    here = pown[n, block(place_of(h - hops_b)), :]
                    bsend[n, h] = (brecv[n, h - 1].astype(F32) + here).astype(BF16)
                    r_b(n, h + 1).start()

        n = s - 1

        @pl.when((n >= 0) & (n < chunks))
        def _():
            r_s(n).wait_recv()
            pown[n] = pown[n] + srecv[n].astype(F32)
            asend[n, 0] = pown[n, block(place_of(hops_a)), :].astype(BF16)
            r_a(n, 1).start()
            bsend[n, 0] = pown[n, block(place_of(-hops_b)), :].astype(BF16)
            r_b(n, 1).start()

        @pl.when(s < chunks)
        def _():
            slot = lax.rem(s + chunks, slots)
            w_down(s, slot, 0).wait()
            w_down(s, slot, 1).wait()
            tile = min(512, wide)
            for j in range(0, wide, tile):
                part[:, j : j + tile] = jnp.dot(
                    act[:, :wide], wbuf[slot, :, j : j + tile], preferred_element_type=F32
                ) + jnp.dot(
                    act[:, wide:], wbuf[slot, :, wide + j : wide + j + tile],
                    preferred_element_type=F32)
            w_start(s + chunks + slots)
            for p in range(chips):
                theirs = part[pl.ds(pl.multiple_of(p * 16 + 8 - 8 * core, 8), 8), :]
                mine = part[pl.ds(pl.multiple_of(p * 16 + 8 * core, 8), 8), :]
                rows = slice(p * 16, p * 16 + 16)
                ssend[s, rows, :] = jnp.concatenate(
                    [theirs[:, :half], theirs[:, half:]], axis=0).astype(BF16)
                pown[s, rows, :] = jnp.concatenate([mine[:, :half], mine[:, half:]], axis=0)
            r_s(s).start()

        return carry

    lax.fori_loop(0, chunks + hops_a + 1, scatter_step, 0)

    swap_x.wait_send()
    swap_i.wait_send()
    for h in range(1, hops_a + 1):
        i_a(h).wait_send()
    for h in range(1, hops_b + 1):
        i_b(h).wait_send()

    def drain(k, carry):
        g_s(k).wait_send()
        r_s(k).wait_send()
        for h in range(1, hops_a + 1):
            g_a(k, h).wait_send()
            r_a(k, h).wait_send()
        for h in range(1, hops_b + 1):
            g_b(k, h).wait_send()
            r_b(k, h).wait_send()
        return carry

    lax.fori_loop(0, chunks, drain, 0)


def fused(hidden_in, norm_gain, norm_shift, up_weight, up_bias, down_weight, down_bias, active):
    members = lax.axis_size("tp")
    rows, features = hidden_in.shape
    neurons = up_weight.shape[1]
    chips = members // 2
    wide = neurons // 2
    half = wide // 2
    chunks = features // wide
    slots = min(SLOTS, chunks)
    hops_a, hops_b = chips // 2, chips - 1 - chips // 2
    everyone = members * rows
    vmem = pl.BlockSpec(memory_space=pltpu.VMEM)
    hbm = pl.BlockSpec(memory_space=pl.ANY)
    dma = pltpu.SemaphoreType.DMA
    return pl.pallas_call(
        functools.partial(fused_kernel, (chips, chunks, wide, slots)),
        out_shape=jax.ShapeDtypeStruct((rows, features), BF16),
        in_specs=[vmem, vmem, vmem, hbm, vmem, hbm, vmem, vmem],
        out_specs=vmem,
        scratch_shapes=[
            pltpu.VMEM((slots, wide, 2 * wide), BF16),
            pltpu.VMEM((2, chunks, rows, half), F32),
            pltpu.VMEM((chunks, rows, half), F32),
            pltpu.VMEM((rows, 128), F32),
            pltpu.VMEM((rows, 128), F32),
            pltpu.VMEM((chunks, 2, everyone, half), BF16),
            pltpu.VMEM((everyone, 128), BF16),
            pltpu.VMEM((everyone, neurons), F32),
            pltpu.VMEM((everyone, neurons), BF16),
            pltpu.VMEM((everyone, wide), F32),
            pltpu.VMEM((chunks, everyone, half), F32),
            pltpu.VMEM((chunks, everyone, half), BF16),
            pltpu.VMEM((chunks, everyone, half), BF16),
            pltpu.VMEM((chunks, hops_a, 16, half), BF16),
            pltpu.VMEM((chunks, hops_a, 16, half), BF16),
            pltpu.VMEM((chunks, hops_b, 16, half), BF16),
            pltpu.VMEM((chunks, hops_b, 16, half), BF16),
            dma((slots, 2)),
            dma((2,)), dma((2,)),
            dma((chunks, hops_a)), dma((chunks, hops_a)),
            dma((chunks, hops_b)), dma((chunks, hops_b)),
            dma((chunks,)), dma((chunks,)),
            dma((hops_a,)), dma((hops_a,)), dma((hops_b,)), dma((hops_b,)),
            dma((chunks, hops_a)), dma((chunks, hops_a)),
            dma((chunks, hops_b)), dma((chunks, hops_b)),
            dma((chunks,)), dma((chunks,)),
        ],
        compiler_params=pltpu.CompilerParams(
            collective_id=0, has_side_effects=True, vmem_limit_bytes=60 * 1024 * 1024),
        cost_estimate=pl.CostEstimate(
            flops=4 * everyone * features * neurons,
            bytes_accessed=4 * features * neurons, transcendentals=0),
        name="fused_ffn",
    )(
        hidden_in, norm_gain.reshape(1, -1), norm_shift.reshape(1, -1), up_weight,
        up_bias.reshape(1, -1), down_weight, down_bias.reshape(1, -1), active,
    )


def plain(
    hidden_in, norm_gain, norm_shift, up_weight, up_bias, down_weight, down_bias, active
):
    local_blocks = up_weight.shape[1] // BLOCK
    normed = layer_norm(hidden_in, norm_gain, norm_shift)
    rows = lax.all_gather(normed, "tp", axis=0, tiled=True)
    ids = lax.all_gather(active, "tp", axis=0, tiled=True)
    own = lax.axis_index("tp") * local_blocks + jnp.arange(local_blocks, dtype=jnp.int32)
    mask = jnp.any(ids[:, :, None] == own[None, None, :], axis=1)
    preact = jnp.dot(rows, up_weight, preferred_element_type=jnp.float32)
    preact = preact + up_bias.astype(jnp.float32)
    activated = jnp.maximum(preact, 0.0).astype(jnp.bfloat16)
    activated = jnp.where(jnp.repeat(mask, BLOCK, axis=1), activated, 0)
    part = jnp.dot(activated, down_weight, preferred_element_type=jnp.float32)
    summed = lax.psum_scatter(part.astype(jnp.bfloat16), "tp", scatter_dimension=0, tiled=True)
    return (summed.astype(jnp.float32) + down_bias).astype(jnp.bfloat16)


def per_device(*operands):
    hidden_in, up_weight, active = operands[0], operands[3], operands[7]
    features, neurons = up_weight.shape
    members = lax.axis_size("tp")
    fits = (
        members == 16
        and hidden_in.shape[0] == 8
        and active.shape[1] <= 128
        and members * neurons // BLOCK <= 256
        and neurons % 512 == 0
        and features % (neurons // 2) == 0
        and neurons <= 2048
    )
    return fused(*operands) if fits else plain(*operands)


def solution(mesh):
    return jax.shard_map(
        per_device,
        mesh=mesh,
        in_specs=(
            P(("group", "tp"), None),
            P(),
            P(),
            P(None, "tp"),
            P("tp"),
            P("tp", None),
            P(),
            P(("group", "tp"), None),
        ),
        out_specs=P(("group", "tp"), None),
        check_vma=False,
    )
```

```python
import functools

import jax
import jax.numpy as jnp
from jax import lax
from jax.experimental import pallas as pl
from jax.experimental.pallas import tpu as pltpu
from jax.sharding import PartitionSpec as P

BLOCK = 128


def layer_norm(hidden_in, norm_gain, norm_shift):
    values = hidden_in.astype(jnp.float32)
    center = jnp.mean(values, axis=1, keepdims=True)
    spread = jnp.mean((values - center) ** 2, axis=1, keepdims=True)
    scaled = (values - center) / jnp.sqrt(spread + 1e-05)
    return (scaled * norm_gain + norm_shift).astype(jnp.bfloat16)


F32 = jnp.float32
BF16 = jnp.bfloat16
SLOTS = 10
GAP = 3
SIB = 2


def fused_kernel(
    dims, hidden, gain, shift, up_hbm, up_bias, down_hbm, down_bias, active, out,
    wbuf, xn, xs, ids_own, ids_sib, xg, idg, preact, act, part, pown,
    ssend, srecv, asend, arecv, bsend, brecv,
    w_sem, e_send, e_recv, ga_send, ga_recv, gb_send, gb_recv, gs_send, gs_recv,
    ia_send, ia_recv, ib_send, ib_recv, ra_send, ra_recv, rb_send, rb_recv, rs_send, rs_recv,
):
    chips, chunks, wide, slots = dims
    half = wide // 2
    hops_a, hops_b = chips // 2, chips - 1 - chips // 2
    deep = chips // 2
    me = lax.axis_index("tp")
    core = lax.rem(me, 2)
    chip = me // 2
    side = lax.rem(chip, 2)
    step_z = chip // 2
    pos = step_z + side * (2 * deep - 1 - 2 * step_z)
    turn = 1 - 2 * core

    def device_at(place):
        s = place // deep
        z = place + s * (2 * deep - 1 - 2 * place)
        return (z * 2 + s) * 2 + core

    def place_of(offset):
        return lax.rem(pos + turn * offset + 2 * chips, chips)

    to_a = device_at(place_of(1))
    to_b = device_at(place_of(-1))
    sibling = chip * 2 + 1 - core

    def send(src, dst, s_sem, r_sem, target):
        return pltpu.make_async_remote_copy(
            src_ref=src, dst_ref=dst, send_sem=s_sem, recv_sem=r_sem,
            device_id={"tp": target}, device_id_type=pl.DeviceIdType.MESH,
        )

    def block(place):
        return pl.ds(pl.multiple_of(place * 16, 16), 16)

    def w_up(g, slot, j):
        rows = pl.ds(pl.multiple_of(g * wide, wide), wide)
        return pltpu.make_async_copy(
            up_hbm.at[rows, pl.ds(j * wide, wide)],
            wbuf.at[slot, :, pl.ds(j * wide, wide)], w_sem.at[slot, j])

    def w_down(n, slot, j):
        cols = pl.ds(pl.multiple_of(n * wide, wide), wide)
        return pltpu.make_async_copy(
            down_hbm.at[pl.ds(j * wide, wide), cols],
            wbuf.at[slot, :, pl.ds(j * wide, wide)], w_sem.at[slot, j])

    def w_start(g):
        slot = lax.rem(g, slots)

        @pl.when(g < chunks)
        def _():
            w_up(g, slot, 0).start()
            w_up(g, slot, 1).start()

        @pl.when((g >= chunks) & (g < 2 * chunks))
        def _():
            w_down(g - chunks, slot, 0).start()
            w_down(g - chunks, slot, 1).start()

    for g in range(slots):
        for j in range(2):
            w_up(g, g, j).start()

    barrier = pltpu.get_barrier_semaphore()
    for other in (to_a, to_b, sibling):
        pl.semaphore_signal(
            barrier, inc=1, device_id={"tp": other}, device_id_type=pl.DeviceIdType.MESH)

    values = hidden[...].astype(F32)
    center = jnp.mean(values, axis=1, keepdims=True)
    spread = jnp.mean((values - center) ** 2, axis=1, keepdims=True)
    root = jnp.sqrt(spread + 1e-05)
    for k in range(chunks):
        for h in range(2):
            cols = slice(k * wide + h * half, k * wide + h * half + half)
            scaled = (hidden[:, cols].astype(F32) - center) / root
            xn[h, k] = (scaled * gain[:, cols] + shift[:, cols]).astype(BF16).astype(F32)
    ids_own[...] = jnp.full(ids_own.shape, -1.0, F32)
    ids_own[:, : active.shape[1]] = active[...].astype(F32)
    preact[...] = jnp.zeros(preact.shape, F32)
    pl.semaphore_wait(barrier, 3)
    swap_x = send(xn.at[1 - core], xs, e_send.at[0], e_recv.at[0], sibling)
    swap_i = send(ids_own, ids_sib, e_send.at[1], e_recv.at[1], sibling)
    swap_x.start()
    swap_i.start()
    swap_x.wait_recv()
    swap_i.wait_recv()

    def pair(mine, theirs):
        first = jnp.where(core == 0, mine, theirs)
        second = jnp.where(core == 0, theirs, mine)
        return jnp.concatenate([first, second], axis=0).astype(BF16)

    idg[block(pos), :] = pair(ids_own[...], ids_sib[...])

    def g_a(k, h):
        ref = xg.at[k, core, block(place_of(-(h - 1))), :]
        return send(ref, ref, ga_send.at[k, h - 1], ga_recv.at[k, h - 1], to_a)

    def g_b(k, h):
        ref = xg.at[k, core, block(place_of(h - 1)), :]
        return send(ref, ref, gb_send.at[k, h - 1], gb_recv.at[k, h - 1], to_b)

    def i_a(h):
        ref = idg.at[block(place_of(-(h - 1))), :]
        return send(ref, ref, ia_send.at[h - 1], ia_recv.at[h - 1], to_a)

    def i_b(h):
        ref = idg.at[block(place_of(h - 1)), :]
        return send(ref, ref, ib_send.at[h - 1], ib_recv.at[h - 1], to_b)

    def g_s(k):
        ref = xg.at[k, core]
        return send(ref, ref, gs_send.at[k], gs_recv.at[k], sibling)

    def gather_step(s, carry):
        @pl.when(s < chunks)
        def _():
            xg[s, core, block(pos), :] = pair(xn[core, s], xs[s])
            g_a(s, 1).start()
            g_b(s, 1).start()

        @pl.when(s == 0)
        def _():
            i_a(1).start()
            i_b(1).start()

        for h in range(1, hops_a + 1):
            k = s - GAP * h

            @pl.when((k >= 0) & (k < chunks))
            def _():
                g_a(k, h).wait_recv()
                if h < hops_a:
                    g_a(k, h + 1).start()
                if h <= hops_b:
                    g_b(k, h).wait_recv()
                if h < hops_b:
                    g_b(k, h + 1).start()
                if h == hops_a:
                    g_s(k).start()

            @pl.when(k == 0)
            def _():
                i_a(h).wait_recv()
                if h < hops_a:
                    i_a(h + 1).start()
                if h <= hops_b:
                    i_b(h).wait_recv()
                if h < hops_b:
                    i_b(h + 1).start()

        k = s - GAP * hops_a - SIB

        @pl.when(k >= 0)
        def _():
            g_s(k).wait_recv()
            slot = lax.rem(k, slots)
            w_up(k, slot, 0).wait()
            w_up(k, slot, 1).wait()
            tile = min(512, wide)
            for j in range(0, 2 * wide, tile):
                cols = slice(j, j + tile)
                preact[:, cols] += jnp.dot(
                    xg[k, 0], wbuf[slot, :half, cols], preferred_element_type=F32
                ) + jnp.dot(xg[k, 1], wbuf[slot, half:, cols], preferred_element_type=F32)
            w_start(k + slots)

        return carry

    lax.fori_loop(0, chunks + GAP * hops_a + SIB, gather_step, 0)

    ids = idg[...].astype(F32)
    for b in range(2 * wide // BLOCK):
        cols = slice(b * BLOCK, b * BLOCK + BLOCK)
        name = (me * (2 * wide // BLOCK) + b).astype(F32)
        named = jnp.max(jnp.where(ids == name, 1.0, 0.0), axis=1, keepdims=True)
        value = jnp.maximum(preact[:, cols] + up_bias[:, cols].astype(F32), 0.0)
        act[:, cols] = (value * named).astype(BF16)

    def r_s(n):
        return send(ssend.at[n], srecv.at[n], rs_send.at[n], rs_recv.at[n], sibling)

    def r_a(n, h):
        return send(asend.at[n, h - 1], arecv.at[n, h - 1], ra_send.at[n, h - 1],
                    ra_recv.at[n, h - 1], to_a)

    def r_b(n, h):
        return send(bsend.at[n, h - 1], brecv.at[n, h - 1], rb_send.at[n, h - 1],
                    rb_recv.at[n, h - 1], to_b)

    def scatter_step(s, carry):
        n = s - GAP * hops_a - SIB

        @pl.when(n >= 0)
        def _():
            r_a(n, hops_a).wait_recv()
            r_b(n, hops_b).wait_recv()
            total = pown[n, block(pos), :] + arecv[n, hops_a - 1].astype(F32)
            total = total + brecv[n, hops_b - 1].astype(F32)
            for h in range(2):
                cols = pl.ds(pl.multiple_of(n * wide + h * half, half), half)
                out[:, cols] = (total[8 * h : 8 * h + 8] + down_bias[:, cols]).astype(BF16)

        for h in range(hops_a - 1, 0, -1):
            n = s - SIB - GAP * h

            @pl.when((n >= 0) & (n < chunks))
            def _():
                r_a(n, h).wait_recv()
                here = pown[n, block(place_of(hops_a - h)), :]
                asend[n, h] = (arecv[n, h - 1].astype(F32) + here).astype(BF16)
                r_a(n, h + 1).start()
                if h < hops_b:
                    r_b(n, h).wait_recv()
                    here = pown[n, block(place_of(h - hops_b)), :]
                    bsend[n, h] = (brecv[n, h - 1].astype(F32) + here).astype(BF16)
                    r_b(n, h + 1).start()

        n = s - SIB

        @pl.when((n >= 0) & (n < chunks))
        def _():
            r_s(n).wait_recv()
            pown[n] = pown[n] + srecv[n].astype(F32)
            asend[n, 0] = pown[n, block(place_of(hops_a)), :].astype(BF16)
            r_a(n, 1).start()
            bsend[n, 0] = pown[n, block(place_of(-hops_b)), :].astype(BF16)
            r_b(n, 1).start()

        @pl.when(s < chunks)
        def _():
            slot = lax.rem(s + chunks, slots)
            w_down(s, slot, 0).wait()
            w_down(s, slot, 1).wait()
            tile = min(512, wide)
            for j in range(0, wide, tile):
                part[:, j : j + tile] = jnp.dot(
                    act[:, :wide], wbuf[slot, :, j : j + tile], preferred_element_type=F32
                ) + jnp.dot(
                    act[:, wide:], wbuf[slot, :, wide + j : wide + j + tile],
                    preferred_element_type=F32)
            w_start(s + chunks + slots)
            for p in range(chips):
                theirs = part[pl.ds(pl.multiple_of(p * 16 + 8 - 8 * core, 8), 8), :]
                mine = part[pl.ds(pl.multiple_of(p * 16 + 8 * core, 8), 8), :]
                rows = slice(p * 16, p * 16 + 16)
                ssend[s, rows, :] = jnp.concatenate(
                    [theirs[:, :half], theirs[:, half:]], axis=0).astype(BF16)
                pown[s, rows, :] = jnp.concatenate([mine[:, :half], mine[:, half:]], axis=0)
            r_s(s).start()

        return carry

    lax.fori_loop(0, chunks + GAP * hops_a + SIB, scatter_step, 0)

    swap_x.wait_send()
    swap_i.wait_send()
    for h in range(1, hops_a + 1):
        i_a(h).wait_send()
    for h in range(1, hops_b + 1):
        i_b(h).wait_send()

    def drain(k, carry):
        g_s(k).wait_send()
        r_s(k).wait_send()
        for h in range(1, hops_a + 1):
            g_a(k, h).wait_send()
            r_a(k, h).wait_send()
        for h in range(1, hops_b + 1):
            g_b(k, h).wait_send()
            r_b(k, h).wait_send()
        return carry

    lax.fori_loop(0, chunks, drain, 0)


def fused(hidden_in, norm_gain, norm_shift, up_weight, up_bias, down_weight, down_bias, active):
    members = lax.axis_size("tp")
    rows, features = hidden_in.shape
    neurons = up_weight.shape[1]
    chips = members // 2
    wide = neurons // 2
    half = wide // 2
    chunks = features // wide
    slots = min(SLOTS, chunks)
    hops_a, hops_b = chips // 2, chips - 1 - chips // 2
    everyone = members * rows
    vmem = pl.BlockSpec(memory_space=pltpu.VMEM)
    hbm = pl.BlockSpec(memory_space=pl.ANY)
    dma = pltpu.SemaphoreType.DMA
    return pl.pallas_call(
        functools.partial(fused_kernel, (chips, chunks, wide, slots)),
        out_shape=jax.ShapeDtypeStruct((rows, features), BF16),
        in_specs=[vmem, vmem, vmem, hbm, vmem, hbm, vmem, vmem],
        out_specs=vmem,
        scratch_shapes=[
            pltpu.VMEM((slots, wide, 2 * wide), BF16),
            pltpu.VMEM((2, chunks, rows, half), F32),
            pltpu.VMEM((chunks, rows, half), F32),
            pltpu.VMEM((rows, 128), F32),
            pltpu.VMEM((rows, 128), F32),
            pltpu.VMEM((chunks, 2, everyone, half), BF16),
            pltpu.VMEM((everyone, 128), BF16),
            pltpu.VMEM((everyone, neurons), F32),
            pltpu.VMEM((everyone, neurons), BF16),
            pltpu.VMEM((everyone, wide), F32),
            pltpu.VMEM((chunks, everyone, half), F32),
            pltpu.VMEM((chunks, everyone, half), BF16),
            pltpu.VMEM((chunks, everyone, half), BF16),
            pltpu.VMEM((chunks, hops_a, 16, half), BF16),
            pltpu.VMEM((chunks, hops_a, 16, half), BF16),
            pltpu.VMEM((chunks, hops_b, 16, half), BF16),
            pltpu.VMEM((chunks, hops_b, 16, half), BF16),
            dma((slots, 2)),
            dma((2,)), dma((2,)),
            dma((chunks, hops_a)), dma((chunks, hops_a)),
            dma((chunks, hops_b)), dma((chunks, hops_b)),
            dma((chunks,)), dma((chunks,)),
            dma((hops_a,)), dma((hops_a,)), dma((hops_b,)), dma((hops_b,)),
            dma((chunks, hops_a)), dma((chunks, hops_a)),
            dma((chunks, hops_b)), dma((chunks, hops_b)),
            dma((chunks,)), dma((chunks,)),
        ],
        compiler_params=pltpu.CompilerParams(
            collective_id=0, has_side_effects=True, vmem_limit_bytes=60 * 1024 * 1024),
        cost_estimate=pl.CostEstimate(
            flops=4 * everyone * features * neurons,
            bytes_accessed=4 * features * neurons, transcendentals=0),
        name="fused_ffn",
    )(
        hidden_in, norm_gain.reshape(1, -1), norm_shift.reshape(1, -1), up_weight,
        up_bias.reshape(1, -1), down_weight, down_bias.reshape(1, -1), active,
    )


def plain(
    hidden_in, norm_gain, norm_shift, up_weight, up_bias, down_weight, down_bias, active
):
    local_blocks = up_weight.shape[1] // BLOCK
    normed = layer_norm(hidden_in, norm_gain, norm_shift)
    rows = lax.all_gather(normed, "tp", axis=0, tiled=True)
    ids = lax.all_gather(active, "tp", axis=0, tiled=True)
    own = lax.axis_index("tp") * local_blocks + jnp.arange(local_blocks, dtype=jnp.int32)
    mask = jnp.any(ids[:, :, None] == own[None, None, :], axis=1)
    preact = jnp.dot(rows, up_weight, preferred_element_type=jnp.float32)
    preact = preact + up_bias.astype(jnp.float32)
    activated = jnp.maximum(preact, 0.0).astype(jnp.bfloat16)
    activated = jnp.where(jnp.repeat(mask, BLOCK, axis=1), activated, 0)
    part = jnp.dot(activated, down_weight, preferred_element_type=jnp.float32)
    summed = lax.psum_scatter(part.astype(jnp.bfloat16), "tp", scatter_dimension=0, tiled=True)
    return (summed.astype(jnp.float32) + down_bias).astype(jnp.bfloat16)


def per_device(*operands):
    hidden_in, up_weight, active = operands[0], operands[3], operands[7]
    features, neurons = up_weight.shape
    members = lax.axis_size("tp")
    fits = (
        members == 16
        and hidden_in.shape[0] == 8
        and active.shape[1] <= 128
        and members * neurons // BLOCK <= 256
        and neurons % 512 == 0
        and features % (neurons // 2) == 0
        and neurons <= 2048
    )
    return fused(*operands) if fits else plain(*operands)


def solution(mesh):
    return jax.shard_map(
        per_device,
        mesh=mesh,
        in_specs=(
            P(("group", "tp"), None),
            P(),
            P(),
            P(None, "tp"),
            P("tp"),
            P("tp", None),
            P(),
            P(("group", "tp"), None),
        ),
        out_specs=P(("group", "tp"), None),
        check_vma=False,
    )
```
